32 devices in a mesh: section: 2 (over x), slab: 16 (over z, y, core).
Axes of the slice: x: 2, y: 2, z: 4, core: 2. Of those that a mesh axis runs over, the one named last changes fastest.
Arguments:
- fields: bfloat16 [2, 4, 32, 128, 128], P('section', None, 'slab'), may hold values from -6 to 6
- lift_weight: bfloat16 [4, 32], replicated, may hold values from -3 to 3
- lift_bias: bfloat16 [32], replicated, may hold values from -3 to 3
- spectral_weight: bfloat16 [2, 2, 32, 32, 16384], P(None, None, None, 'section', 'slab'), may hold values from -0.75 to 0.75
- bypass_weight: bfloat16 [2, 32, 32], replicated, may hold values from -1 to 1
- bypass_bias: bfloat16 [2, 32], replicated, may hold values from -3 to 3
Outputs:
- features: bfloat16 [2, 32, 32, 128, 128], P('section', None, 'slab')
The draws below stay inside these ranges and needn't reach their ends.
All inputs are finite; a program needn't handle non-finite values.
Results may differ from the reference program's by a relative error of at most 0.015.
Values may be sent and summed in bfloat16 or wider, within the bound.
A program may use at most 64 MiB of HBM per device.

```python
import math
import jax
import jax.numpy as jnp
from jax import lax

C = 32
K = 16
CIN = 4
NX = 128
NY = 128
LAYERS = 2
M = 2
NZ = 32


def block_levels(stream_key, shape, pieces, smallest, high):
    loudness, own = 1.0, jax.random.fold_in(stream_key, 6)
    for position, blocks in pieces:
        heights = jnp.exp(jax.random.uniform(jax.random.fold_in(own, position), (blocks,), jnp.float32, smallest / len(pieces), high / len(pieces)))
        loudness = loudness * jnp.repeat(heights, shape[position] // blocks).reshape([-1 if axis == position else 1 for axis in range(len(shape))])
    return loudness


def normal_values(rng, shape, scale, bound, shards=(), held_as=jnp.bfloat16):
    level = block_levels(rng, shape, shards, -0.22, 0.18) if shards else 1.0
    result = jax.random.normal(rng, shape, jnp.float32) * scale * level
    return jnp.minimum(jnp.maximum(result, -bound), bound).astype(held_as)


def setup_inputs(seed: int = 0) -> dict:
    arg_keys = jax.random.split(jax.random.key(seed), 7)
    fields = normal_values(arg_keys[0], (M, CIN, NZ, NX, NY), 1.0, 6.0, ((0, 2), (2, 16)))
    lift_weight = normal_values(arg_keys[1], (CIN, C), CIN ** -0.5, 3.0)
    lift_bias = normal_values(arg_keys[2], (C,), 0.5, 3.0)
    spectral_weight = normal_values(arg_keys[3], (LAYERS, 2, C, C, 4 * K * K * K), (2 * C) ** -0.5, 0.75, ((3, 2), (4, 16)))
    bypass_weight = normal_values(arg_keys[4], (LAYERS, C, C), C ** -0.5, 1.0)
    bypass_bias = normal_values(arg_keys[5], (LAYERS, C), 0.5, 3.0)
    return dict(fields=fields, lift_weight=lift_weight, lift_bias=lift_bias, spectral_weight=spectral_weight, bypass_weight=bypass_weight, bypass_bias=bypass_bias)


def signed_list(count):
    base = jnp.arange(2 * count, dtype=jnp.int32)
    return jnp.where(base < count, base, base - 2 * count)

def tables(freqs, length, first, span):
    freq = (freqs % length)[:, None]
    where = first + jnp.arange(span, dtype=jnp.int32)[None, :]
    phase = (freq * where % length).astype(jnp.float32) * (2.0 * math.pi / length)
    return (jnp.cos(phase).astype(jnp.bfloat16), jnp.sin(phase).astype(jnp.bfloat16))

def forward_pair(freqs, length):
    cosine, sine = tables(freqs, length, 0, length)
    return jnp.concatenate([cosine, -sine], axis=0).T

def product(form, left, right):
    return jnp.einsum(form, left.astype(jnp.float32), right.astype(jnp.float32), precision=lax.Precision.HIGHEST)

def one_variant(fields, lift_weight, lift_bias, spectral_weight, bypass_weight, bypass_bias):
    half = 2 * K
    modes_xy = half * half
    hidden = (product('czxy,cd->dzxy', fields, lift_weight) + lift_bias.astype(jnp.float32)[:, None, None, None]).astype(jnp.bfloat16)
    xy_list = signed_list(K)
    z_list = jnp.arange(K, dtype=jnp.int32)
    table_y = forward_pair(xy_list, NY)
    table_x = forward_pair(xy_list, NX)
    table_z = forward_pair(z_list, NZ)
    doubling = jnp.where(z_list == 0, 1.0, 2.0).astype(jnp.bfloat16)[:, None]
    cos_z, sin_z = tables(z_list, NZ, 0, NZ)
    cos_z = cos_z * doubling
    sin_z = sin_z * doubling
    cos_x, sin_x = tables(xy_list, NX, 0, NX)
    cos_y, sin_y = tables(xy_list, NY, 0, NY)
    back_y = jnp.concatenate([cos_y, -sin_y], axis=0)
    keep = (jnp.arange(modes_xy * K, dtype=jnp.int32) != 0).astype(jnp.float32).reshape(modes_xy, K)
    for layer in range(LAYERS):
        along_y = (product('czxy,yq->czxq', hidden, table_y) / math.sqrt(NY)).astype(jnp.bfloat16)
        both = product('czxq,xp->czpq', along_y, table_x)
        spec_real = both[:, :, :half, :half] - both[:, :, half:, half:]
        spec_imag = both[:, :, :half, half:] + both[:, :, half:, :half]
        spectrum = (jnp.stack([spec_real, spec_imag], 1) / math.sqrt(NX)).astype(jnp.bfloat16)
        spectrum = spectrum.reshape(C, 2, NZ, modes_xy)
        along_z = product('crzj,zq->crjq', spectrum, table_z)
        mode_real = (along_z[:, 0, :, :K] - along_z[:, 1, :, K:]) / math.sqrt(NZ) * keep
        mode_imag = (along_z[:, 1, :, :K] + along_z[:, 0, :, K:]) / math.sqrt(NZ) * keep
        weights = spectral_weight[layer].astype(jnp.float32).reshape(2, C, C, modes_xy, K)
        mixed_real = product('ijk,iojk->ojk', mode_real, weights[0]) - product('ijk,iojk->ojk', mode_imag, weights[1])
        mixed_imag = product('ijk,iojk->ojk', mode_imag, weights[0]) + product('ijk,iojk->ojk', mode_real, weights[1])
        mixed = jnp.stack([mixed_real, mixed_imag], 1).astype(jnp.bfloat16)
        plain = product('crjk,kz->crjz', mixed, cos_z)
        skewed = product('crjk,kz->crjz', mixed, sin_z)
        planes_back = (jnp.stack([plain[:, 0] - skewed[:, 1], skewed[:, 0] + plain[:, 1]], 1) * 0.25).astype(jnp.bfloat16)
        grid = planes_back.reshape(C, 2, half, half, NZ)
        plain = product('crpqz,px->czxrq', grid, cos_x)
        skewed = product('crpqz,px->czxrq', grid, sin_x)
        along_x = (jnp.concatenate([plain[:, :, :, 0] - skewed[:, :, :, 1], skewed[:, :, :, 0] + plain[:, :, :, 1]], -1) * 0.125).astype(jnp.bfloat16)
        spectral_field = product('czxq,qy->czxy', along_x, back_y) * 0.125
        bypassed = product('czxy,co->ozxy', hidden, bypass_weight[layer]) + bypass_bias[layer].astype(jnp.float32)[:, None, None, None]
        hidden = jax.nn.gelu(bypassed + spectral_field, approximate=True).astype(jnp.bfloat16)
    return hidden

def reference(fields, lift_weight, lift_bias, spectral_weight, bypass_weight, bypass_bias):

    def single(variant):
        return one_variant(variant, lift_weight, lift_bias, spectral_weight, bypass_weight, bypass_bias)
    return lax.map(single, fields)
```

```python
import functools
import math

import jax
import jax.numpy as jnp
import ml_dtypes
import numpy as np
from jax import lax
from jax.experimental import pallas as pl
from jax.experimental.pallas import tpu as pltpu
from jax.sharding import PartitionSpec as P

K = 16
LAYERS = 2


def signed_list(count):
    base = jnp.arange(2 * count, dtype=jnp.int32)
    return jnp.where(base < count, base, base - 2 * count)


def tables(freqs, length, span):
    freq = (freqs % length)[:, None]
    where = jnp.arange(span, dtype=jnp.int32)[None, :]
    phase = (freq * where % length).astype(jnp.float32) * (2.0 * math.pi / length)
    return (jnp.cos(phase).astype(jnp.bfloat16), jnp.sin(phase).astype(jnp.bfloat16))


def forward_pair(freqs, length):
    cosine, sine = tables(freqs, length, length)
    return jnp.concatenate([cosine, -sine], axis=0).T


def inverse_planes(mixed, cosine, sine):
    plain = jnp.einsum("mcrjk,kz->mcrjz", mixed, cosine, preferred_element_type=jnp.float32)
    skewed = jnp.einsum("mcrjk,kz->mcrjz", mixed, sine, preferred_element_type=jnp.float32)
    joined = jnp.stack([plain[:, :, 0] - skewed[:, :, 1], skewed[:, :, 0] + plain[:, :, 1]], 2)
    return (joined * 0.25).astype(jnp.bfloat16)


def on_device(fields, lift_weight, lift_bias, spectral_weight, bypass_weight, bypass_bias):
    slabs = lax.axis_size("slab")
    batch, inputs, depth, rows_x, rows_y = fields.shape
    width = lift_weight.shape[1]
    whole_z = depth * slabs
    half = 2 * K
    modes_xy = half * half
    owned = modes_xy // slabs
    place = lax.axis_index("slab")
    hidden = (
        jnp.einsum("mczxy,cd->mdzxy", fields, lift_weight, preferred_element_type=jnp.float32)
        + lift_bias.astype(jnp.float32)[None, :, None, None, None]
    ).astype(jnp.bfloat16)
    xy_list = signed_list(K)
    z_list = jnp.arange(K, dtype=jnp.int32)
    table_y = forward_pair(xy_list, rows_y)
    table_x = forward_pair(xy_list, rows_x)
    table_z = forward_pair(z_list, whole_z)
    doubling = jnp.where(z_list == 0, 1.0, 2.0).astype(jnp.bfloat16)[:, None]
    cos_z, sin_z = tables(z_list, whole_z, whole_z)
    cos_z = cos_z * doubling
    sin_z = sin_z * doubling
    cos_x, sin_x = tables(xy_list, rows_x, rows_x)
    cos_y, sin_y = tables(xy_list, rows_y, rows_y)
    back_y = jnp.concatenate([cos_y, -sin_y], axis=0)
    combined_x = jnp.stack([jnp.stack([cos_x, sin_x], 1), jnp.stack([-sin_x, cos_x], 1)], 0)
    index_modes = place * (owned * K) + jnp.arange(owned * K, dtype=jnp.int32)
    keep = (index_modes != 0).astype(jnp.float32).reshape(owned, K)
    scale_z = 1.0 / math.sqrt(whole_z)
    highest = lax.Precision.HIGHEST
    for layer in range(LAYERS):
        spectral = lax.all_gather(spectral_weight[layer], "section", axis=2, tiled=True)
        along_y = (
            jnp.dot(hidden, table_y, preferred_element_type=jnp.float32) / math.sqrt(rows_y)
        ).astype(jnp.bfloat16)
        both = jnp.einsum("mczxq,xp->mczpq", along_y, table_x, preferred_element_type=jnp.float32)
        spec_real = both[..., :half, :half] - both[..., half:, half:]
        spec_imag = both[..., :half, half:] + both[..., half:, :half]
        spectrum = (jnp.stack([spec_real, spec_imag], 2) / math.sqrt(rows_x)).astype(jnp.bfloat16)
        spectrum = spectrum.reshape(batch, width, 2, depth, modes_xy).transpose(0, 1, 2, 4, 3)
        gathered = lax.all_to_all(spectrum, "slab", split_axis=3, concat_axis=4, tiled=True)
        along_z = jnp.einsum(
            "mcrjz,zq->mcrjq", gathered, table_z, preferred_element_type=jnp.float32
        )
        mode_real = (along_z[:, :, 0, :, :K] - along_z[:, :, 1, :, K:]) * scale_z * keep
        mode_imag = (along_z[:, :, 1, :, :K] + along_z[:, :, 0, :, K:]) * scale_z * keep
        weights = spectral.astype(jnp.float32).reshape(2, width, width, owned, K)
        mixed_real = jnp.einsum(
            "mijk,iojk->mojk", mode_real, weights[0], precision=highest
        ) - jnp.einsum("mijk,iojk->mojk", mode_imag, weights[1], precision=highest)
        mixed_imag = jnp.einsum(
            "mijk,iojk->mojk", mode_imag, weights[0], precision=highest
        ) + jnp.einsum("mijk,iojk->mojk", mode_real, weights[1], precision=highest)
        mixed = jnp.stack([mixed_real, mixed_imag], 2).astype(jnp.bfloat16)
        every_plane = inverse_planes(mixed, cos_z, sin_z)
        planes_back = lax.all_to_all(every_plane, "slab", split_axis=4, concat_axis=3, tiled=True)
        grid = planes_back.reshape(batch, width, 2, half, half, depth)
        along_x = (
            jnp.einsum("mcrpqz,rpsx->mczxsq", grid, combined_x, preferred_element_type=jnp.float32)
            * 0.125
        ).astype(jnp.bfloat16)
        along_x = along_x.reshape(batch, width, depth, rows_x, 2 * half)
        spectral_field = jnp.dot(along_x, back_y, preferred_element_type=jnp.float32) * 0.125
        bypassed = (
            jnp.einsum(
                "mczxy,co->mozxy", hidden, bypass_weight[layer], preferred_element_type=jnp.float32
            )
            + bypass_bias[layer].astype(jnp.float32)[None, :, None, None, None]
        )
        hidden = jax.nn.gelu(bypassed + spectral_field, approximate=True).astype(jnp.bfloat16)
    return hidden


BF = ml_dtypes.bfloat16


def host_tables(freqs, length):
    phase = (freqs[:, None] * np.arange(length)[None, :]) % length * (2.0 * math.pi / length)
    return (
        np.cos(phase).astype(BF).astype(np.float64),
        np.sin(phase).astype(BF).astype(np.float64),
    )


def constants(slabs, depth, nx, ny, width):
    whole_z = slabs * depth
    half = 2 * K
    lift = half // slabs
    groups = width // 4
    signed = np.where(np.arange(half) < K, np.arange(half), np.arange(half) - half)
    cy, sy = host_tables(signed, ny)
    cx, sx = host_tables(signed, nx)
    cz, sz = host_tables(np.arange(K), whole_z)
    eye4 = np.eye(4)
    fwd_y = np.concatenate([np.kron(eye4, cy.T), np.kron(eye4, -sy.T)], 1)
    fwd_x = np.block([[cx, sx], [-sx, cx]])
    rows = groups * depth * 2
    order = np.arange(rows * half).reshape(rows, slabs, lift).transpose(1, 0, 2).ravel()
    spread = np.eye(rows * half)[order]
    collect = spread.T
    pair = np.stack([np.stack([cz, sz], 1), np.stack([-sz, cz], 1)], 0)
    pair = pair.reshape(2, K, 2, slabs, depth)
    fwd_z = np.einsum("akbsd,gh,pq->gpakshdbq", pair, np.eye(groups), np.eye(lift))
    fwd_z = fwd_z.reshape(groups * lift * 2 * K, slabs * rows * lift)
    tile = np.kron(np.eye(8), np.tile(np.eye(K), (1, half)))
    total = np.kron(np.eye(width), np.ones((1, half)))
    double = np.where(np.arange(K) == 0, 1.0, 2.0)[:, None]
    dz, ez = cz * double, sz * double
    back = np.stack([np.stack([dz, -ez], 0), np.stack([ez, dz], 0)], 0)
    back = back.reshape(2, 2, K, slabs, depth).transpose(3, 4, 0, 1, 2)
    back_z = np.broadcast_to(back[:, :, :, :, None, :], (slabs, depth, 2, 2, half, K))
    back_z = back_z.reshape(whole_z * 2, 2 * half * K).T
    order = np.arange(groups * lift * whole_z * 2).reshape(groups, lift, slabs, depth, 2)
    order = order.transpose(2, 0, 3, 4, 1).ravel()
    leave = np.eye(order.size)[order]
    back_x = np.block([[cx.T, -sx.T], [sx.T, cx.T]])
    back_y = np.concatenate([np.kron(eye4, cy), np.kron(eye4, -sy)], 0)
    named = dict(
        fwd_y=fwd_y, fwd_x=fwd_x, spread=spread, collect=collect, fwd_z=fwd_z, tile=tile,
        total=total, expand=total.T, back_z=back_z, leave=leave, back_x=back_x, back_y=back_y,
    )
    return {name: np.ascontiguousarray(value).astype(BF) for name, value in named.items()}


def mm(a, b):
    return jnp.dot(a, b, preferred_element_type=jnp.float32)


def mask_of(half):
    row = lax.broadcasted_iota(jnp.int32, (4 * half, half * K), 0) % half
    column = lax.broadcasted_iota(jnp.int32, (4 * half, half * K), 1) // K
    return row == column


def lift_body(fields, kron, bias, hidden):
    width, depth, nx, ny = hidden.shape
    for z in range(depth):
        for g in range(nx // 16):
            block = fields[:, z, g * 16 : g * 16 + 16, :].reshape(-1, ny)
            value = mm(kron[...], block).reshape(width, 16, ny) + bias[...]
            hidden[:, z, g * 16 : g * 16 + 16, :] = value.astype(jnp.bfloat16)


def forward_body(hidden, fwd_y, fwd_x, spread, local, out):
    width, depth, nx, ny = hidden.shape
    for g in range(width // 4):
        for z in range(depth):
            block = jnp.concatenate([hidden[4 * g + c, z] for c in range(4)], axis=1)
            along = (mm(block, fwd_y[...]) * (1.0 / math.sqrt(ny))).astype(jnp.bfloat16)
            lanes = along.shape[1] // 2
            along = jnp.concatenate([along[:, :lanes], along[:, lanes:]], axis=0)
            spec = mm(fwd_x[...], along) * (1.0 / math.sqrt(nx))
            at = (g * depth + z) * spec.shape[0]
            local[at : at + spec.shape[0], :] = spec.astype(jnp.bfloat16)
    out[...] = mm(spread[...], local[...]).astype(jnp.bfloat16)


def modes_body(place, got, fwd_z, tile, total, modes, held, scale):
    half = 2 * K
    lanes = half * K
    width = modes.shape[1]
    lift = modes.shape[2] // lanes
    mask = mask_of(half)
    flat = (mm(fwd_z[...], got[...]) * scale).T.astype(jnp.bfloat16)
    per = lift * 2
    for b in range(flat.shape[1] // 128):
        wide = mm(flat[:, b * 128 : b * 128 + 128], tile[...])
        for e in range(8):
            g, pr = divmod(b * 8 + e, per)
            piece = jnp.where(mask, wide[:, e * lanes : (e + 1) * lanes], 0.0)
            held[pr, g * 128 : g * 128 + 128, :] = piece.astype(jnp.bfloat16)
    for p in range(lift):
        for r in range(2):
            value = mm(total[...], held[p * 2 + r])
            if p == 0:
                lane = lax.broadcasted_iota(jnp.int32, value.shape, 1)
                value = jnp.where(lane + place == 0, 0.0, value)
            modes[r, :, p * lanes : (p + 1) * lanes] = value.astype(jnp.bfloat16)


def mix_body(modes, weights, mixed):
    variants, _, width, lanes = modes.shape
    step = 256
    for b in range(lanes // step):
        at = slice(b * step, (b + 1) * step)
        rows = [[modes[m, r, :, at].astype(jnp.float32) for r in range(2)] for m in range(variants)]
        sums = [[0.0, 0.0] for _ in range(variants)]
        for i in range(width):
            wr = weights[0, i, :, at].astype(jnp.float32)
            wi = weights[1, i, :, at].astype(jnp.float32)
            for m in range(variants):
                real, imag = rows[m][0][i : i + 1], rows[m][1][i : i + 1]
                sums[m][0] += real * wr - imag * wi
                sums[m][1] += imag * wr + real * wi
        for m in range(variants):
            for r in range(2):
                mixed[m, r, :, at] = sums[m][r].astype(jnp.bfloat16)


def planes_body(mixed, expand, back_z, leave, out, local):
    half = 2 * K
    lanes = half * K
    mask = mask_of(half)
    sections = mixed.shape[0]
    lift = mixed.shape[3] // lanes
    groups = expand.shape[0] // 128
    many = back_z.shape[1]
    wholes = [
        jnp.concatenate([mixed[s, r] for s in range(sections)], axis=0) for r in range(2)
    ]
    for g in range(groups):
        values = []
        for p in range(lift):
            pieces = []
            for r in range(2):
                part = wholes[r][:, p * lanes : (p + 1) * lanes]
                wide = mm(expand[g * 128 : g * 128 + 128, :], part)
                pieces.append(jnp.where(mask, wide, 0.0).astype(jnp.bfloat16))
            values.append(mm(jnp.concatenate(pieces, axis=1), back_z[...]) * 0.25)
        value = jnp.concatenate(values, axis=1).T
        local[g * lift * many : (g + 1) * lift * many, :] = value.astype(jnp.bfloat16)
    out[...] = mm(leave[...], local[...]).astype(jnp.bfloat16)


def bypass_body(hidden, kron, bias, direct):
    width, depth, nx, ny = hidden.shape
    for z in range(depth):
        for g in range(nx // 16):
            block = hidden[:, z, g * 16 : g * 16 + 16, :].reshape(-1, ny)
            value = mm(kron[...], block).reshape(width, 16, ny) + bias[...]
            direct[:, z, g * 16 : g * 16 + 16, :] = value


def backward_body(got, direct, collect, back_x, back_y, local, out):
    width, depth, nx, ny = out.shape
    many = back_x.shape[1]
    local[...] = mm(collect[...], got[...]).astype(jnp.bfloat16)
    for g in range(width // 4):
        for z in range(depth):
            at = (g * depth + z) * many
            along = (mm(back_x[...], local[at : at + many, :]) * 0.125).astype(jnp.bfloat16)
            along = jnp.concatenate([along[:nx], along[nx:]], axis=1)
            field = mm(along, back_y[...]) * 0.125
            for c in range(4):
                value = direct[4 * g + c, z] + field[:, c * ny : (c + 1) * ny]
                inner = value * (0.7978845608028654 + 0.035677408136300125 * (value * value))
                value = 0.5 * value * (1.0 + jnp.tanh(inner))
                out[4 * g + c, z] = value.astype(jnp.bfloat16)


def widen(weight, copies):
    ins, outs = weight.shape

    def rep(n):
        row = lax.broadcasted_iota(jnp.int32, (n * copies, n), 0) // copies
        column = lax.broadcasted_iota(jnp.int32, (n * copies, n), 1)
        return (row == column).astype(jnp.bfloat16)

    def last(a, b):
        return lax.dot_general(a, b, (((1,), (1,)), ((), ())), preferred_element_type=jnp.float32)

    tall = last(rep(outs), weight).astype(jnp.bfloat16)
    wide = last(tall, rep(ins))
    row = lax.broadcasted_iota(jnp.int32, wide.shape, 0) % copies
    column = lax.broadcasted_iota(jnp.int32, wide.shape, 1) % copies
    return jnp.where(row == column, wide, 0.0).astype(jnp.bfloat16)


def start_kernel(fields, lift_weight, lift_bias, fwd_y, fwd_x, spread, hidden, out, kron, local):
    kron[...] = widen(lift_weight[...], 16)
    lift_body(fields, kron, lift_bias, hidden)
    forward_body(hidden, fwd_y, fwd_x, spread, local, out)


def modes_kernel(scale, got, fwd_z, tile, total, modes, held):
    place = lax.axis_index("slab")
    modes_body(place, got, fwd_z, tile, total, modes, held, scale)


def layer_kernel(
    got, hidden, weight, bias, collect, back_x, back_y, fwd_y, fwd_x, spread,
    new, out, kron, direct, local,
):
    kron[...] = widen(weight[...], 16)
    bypass_body(hidden, kron, bias, direct)
    backward_body(got, direct, collect, back_x, back_y, local, new)
    forward_body(new, fwd_y, fwd_x, spread, local, out)


def last_kernel(got, hidden, weight, bias, collect, back_x, back_y, new, kron, direct, local):
    kron[...] = widen(weight[...], 16)
    bypass_body(hidden, kron, bias, direct)
    backward_body(got, direct, collect, back_x, back_y, local, new)


def call(kernel, outs, scratch, *args):
    return pl.pallas_call(
        kernel,
        out_shape=outs,
        in_specs=[pl.BlockSpec(memory_space=pltpu.VMEM)] * len(args),
        out_specs=jax.tree.map(lambda _: pl.BlockSpec(memory_space=pltpu.VMEM), outs),
        scratch_shapes=scratch,
        compiler_params=pltpu.CompilerParams(vmem_limit_bytes=50 * 1024 * 1024),
    )(*args)


def on_device_fast(fields, lift_weight, lift_bias, spectral_weight, bypass_weight, bypass_bias):
    slabs, sections = lax.axis_size("slab"), lax.axis_size("section")
    _, inputs, depth, nx, ny = fields.shape
    width = lift_weight.shape[1]
    half = 2 * K
    owned = half * half // slabs
    bf = jnp.bfloat16
    t = constants(slabs, depth, nx, ny, width)
    t = {name: jnp.asarray(value) for name, value in t.items()}
    rows = width // 4 * depth * 2 * half

    def spread_bias(b):
        return jnp.broadcast_to(b.astype(jnp.float32)[..., None, None], b.shape + (1, ny))

    kron = pltpu.VMEM((width * 16, width * 16), bf)
    local = pltpu.VMEM((rows, 128), bf)
    spec = jax.ShapeDtypeStruct((rows, 128), bf)
    hid = jax.ShapeDtypeStruct((width, depth, nx, ny), bf)
    direct = pltpu.VMEM((width, depth, nx, ny), jnp.float32)
    bias = spread_bias(bypass_bias)
    hidden, out = call(
        start_kernel, (hid, spec), [pltpu.VMEM((width * 16, inputs * 16), bf), local],
        fields[0], lift_weight, spread_bias(lift_bias), t["fwd_y"], t["fwd_x"], t["spread"],
    )
    for layer in range(LAYERS):
        got = lax.all_to_all(out, "slab", split_axis=0, concat_axis=0, tiled=True)
        modes = call(
            functools.partial(modes_kernel, 1.0 / math.sqrt(slabs * depth)),
            jax.ShapeDtypeStruct((2, width, owned * K), bf),
            [pltpu.VMEM((owned // half * 2, width * half, half * K), bf)],
            got, t["fwd_z"], t["tile"], t["total"],
        )
        modes = lax.all_gather(modes, "section", axis=0)
        mixed = call(
            mix_body, jax.ShapeDtypeStruct((sections, 2, width // sections, owned * K), bf), [],
            modes, spectral_weight[layer],
        )
        mixed = lax.all_to_all(mixed, "section", split_axis=0, concat_axis=0, tiled=True)
        planes = call(
            planes_body, spec, [local], mixed, t["expand"], t["back_z"], t["leave"],
        )
        got = lax.all_to_all(planes, "slab", split_axis=0, concat_axis=0, tiled=True)
        if layer < LAYERS - 1:
            hidden, out = call(
                layer_kernel, (hid, spec), [kron, direct, local], got, hidden,
                bypass_weight[layer], bias[layer], t["collect"], t["back_x"], t["back_y"],
                t["fwd_y"], t["fwd_x"], t["spread"],
            )
        else:
            hidden = call(
                last_kernel, hid, [kron, direct, local], got, hidden,
                bypass_weight[layer], bias[layer], t["collect"], t["back_x"], t["back_y"],
            )
    return hidden[None]


def solution(mesh):
    slabs, sections = mesh.shape["slab"], mesh.shape["section"]
    placed = (
        P("section", None, "slab", None, None),
        P(),
        P(),
        P(None, None, None, "section", "slab"),
        P(),
        P(),
    )
    fits = 2 * K % slabs == 0

    def whole(fields, *rest):
        single = fits and fields.shape[0] == sections
        return jax.shard_map(
            on_device_fast if single else on_device,
            mesh=mesh,
            in_specs=placed,
            out_specs=P("section", None, "slab", None, None),
            check_vma=False,
        )(fields, *rest)

    return whole
```

```python
import functools
import math

import jax
import jax.numpy as jnp
import ml_dtypes
import numpy as np
from jax import lax
from jax.experimental import pallas as pl
from jax.experimental.pallas import tpu as pltpu
from jax.sharding import PartitionSpec as P

K = 16
LAYERS = 2


def signed_list(count):
    base = jnp.arange(2 * count, dtype=jnp.int32)
    return jnp.where(base < count, base, base - 2 * count)


def tables(freqs, length, span):
    freq = (freqs % length)[:, None]
    where = jnp.arange(span, dtype=jnp.int32)[None, :]
    phase = (freq * where % length).astype(jnp.float32) * (2.0 * math.pi / length)
    return (jnp.cos(phase).astype(jnp.bfloat16), jnp.sin(phase).astype(jnp.bfloat16))


def forward_pair(freqs, length):
    cosine, sine = tables(freqs, length, length)
    return jnp.concatenate([cosine, -sine], axis=0).T


def inverse_planes(mixed, cosine, sine):
    plain = jnp.einsum("mcrjk,kz->mcrjz", mixed, cosine, preferred_element_type=jnp.float32)
    skewed = jnp.einsum("mcrjk,kz->mcrjz", mixed, sine, preferred_element_type=jnp.float32)
    joined = jnp.stack([plain[:, :, 0] - skewed[:, :, 1], skewed[:, :, 0] + plain[:, :, 1]], 2)
    return (joined * 0.25).astype(jnp.bfloat16)


def on_device(fields, lift_weight, lift_bias, spectral_weight, bypass_weight, bypass_bias):
    slabs = lax.axis_size("slab")
    batch, inputs, depth, rows_x, rows_y = fields.shape
    width = lift_weight.shape[1]
    whole_z = depth * slabs
    half = 2 * K
    modes_xy = half * half
    owned = modes_xy // slabs
    place = lax.axis_index("slab")
    hidden = (
        jnp.einsum("mczxy,cd->mdzxy", fields, lift_weight, preferred_element_type=jnp.float32)
        + lift_bias.astype(jnp.float32)[None, :, None, None, None]
    ).astype(jnp.bfloat16)
    xy_list = signed_list(K)
    z_list = jnp.arange(K, dtype=jnp.int32)
    table_y = forward_pair(xy_list, rows_y)
    table_x = forward_pair(xy_list, rows_x)
    table_z = forward_pair(z_list, whole_z)
    doubling = jnp.where(z_list == 0, 1.0, 2.0).astype(jnp.bfloat16)[:, None]
    cos_z, sin_z = tables(z_list, whole_z, whole_z)
    cos_z = cos_z * doubling
    sin_z = sin_z * doubling
    cos_x, sin_x = tables(xy_list, rows_x, rows_x)
    cos_y, sin_y = tables(xy_list, rows_y, rows_y)
    back_y = jnp.concatenate([cos_y, -sin_y], axis=0)
    combined_x = jnp.stack([jnp.stack([cos_x, sin_x], 1), jnp.stack([-sin_x, cos_x], 1)], 0)
    index_modes = place * (owned * K) + jnp.arange(owned * K, dtype=jnp.int32)
    keep = (index_modes != 0).astype(jnp.float32).reshape(owned, K)
    scale_z = 1.0 / math.sqrt(whole_z)
    highest = lax.Precision.HIGHEST
    for layer in range(LAYERS):
        spectral = lax.all_gather(spectral_weight[layer], "section", axis=2, tiled=True)
        along_y = (
            jnp.dot(hidden, table_y, preferred_element_type=jnp.float32) / math.sqrt(rows_y)
        ).astype(jnp.bfloat16)
        both = jnp.einsum("mczxq,xp->mczpq", along_y, table_x, preferred_element_type=jnp.float32)
        spec_real = both[..., :half, :half] - both[..., half:, half:]
        spec_imag = both[..., :half, half:] + both[..., half:, :half]
        spectrum = (jnp.stack([spec_real, spec_imag], 2) / math.sqrt(rows_x)).astype(jnp.bfloat16)
        spectrum = spectrum.reshape(batch, width, 2, depth, modes_xy).transpose(0, 1, 2, 4, 3)
        gathered = lax.all_to_all(spectrum, "slab", split_axis=3, concat_axis=4, tiled=True)
        along_z = jnp.einsum(
            "mcrjz,zq->mcrjq", gathered, table_z, preferred_element_type=jnp.float32
        )
        mode_real = (along_z[:, :, 0, :, :K] - along_z[:, :, 1, :, K:]) * scale_z * keep
        mode_imag = (along_z[:, :, 1, :, :K] + along_z[:, :, 0, :, K:]) * scale_z * keep
        weights = spectral.astype(jnp.float32).reshape(2, width, width, owned, K)
        mixed_real = jnp.einsum(
            "mijk,iojk->mojk", mode_real, weights[0], precision=highest
        ) - jnp.einsum("mijk,iojk->mojk", mode_imag, weights[1], precision=highest)
        mixed_imag = jnp.einsum(
            "mijk,iojk->mojk", mode_imag, weights[0], precision=highest
        ) + jnp.einsum("mijk,iojk->mojk", mode_real, weights[1], precision=highest)
        mixed = jnp.stack([mixed_real, mixed_imag], 2).astype(jnp.bfloat16)
        every_plane = inverse_planes(mixed, cos_z, sin_z)
        planes_back = lax.all_to_all(every_plane, "slab", split_axis=4, concat_axis=3, tiled=True)
        grid = planes_back.reshape(batch, width, 2, half, half, depth)
        along_x = (
            jnp.einsum("mcrpqz,rpsx->mczxsq", grid, combined_x, preferred_element_type=jnp.float32)
            * 0.125
        ).astype(jnp.bfloat16)
        along_x = along_x.reshape(batch, width, depth, rows_x, 2 * half)
        spectral_field = jnp.dot(along_x, back_y, preferred_element_type=jnp.float32) * 0.125
        bypassed = (
            jnp.einsum(
                "mczxy,co->mozxy", hidden, bypass_weight[layer], preferred_element_type=jnp.float32
            )
            + bypass_bias[layer].astype(jnp.float32)[None, :, None, None, None]
        )
        hidden = jax.nn.gelu(bypassed + spectral_field, approximate=True).astype(jnp.bfloat16)
    return hidden


BF = ml_dtypes.bfloat16


def host_tables(freqs, length):
    phase = (freqs[:, None] * np.arange(length)[None, :]) % length * (2.0 * math.pi / length)
    return (
        np.cos(phase).astype(BF).astype(np.float64),
        np.sin(phase).astype(BF).astype(np.float64),
    )


def constants(slabs, depth, nx, ny, width):
    whole_z = slabs * depth
    half = 2 * K
    lift = half // slabs
    groups = width // 4
    signed = np.where(np.arange(half) < K, np.arange(half), np.arange(half) - half)
    cy, sy = host_tables(signed, ny)
    cx, sx = host_tables(signed, nx)
    cz, sz = host_tables(np.arange(K), whole_z)
    eye4 = np.eye(4)
    fwd_y = np.concatenate([np.kron(eye4, cy.T), np.kron(eye4, -sy.T)], 1)
    fwd_x = np.block([[cx, sx], [-sx, cx]])
    rows = groups * depth * 2
    order = np.arange(rows * half).reshape(rows, slabs, lift).transpose(1, 0, 2).ravel()
    spread = np.eye(rows * half)[order]
    collect = spread.T
    pair = np.stack([np.stack([cz, sz], 1), np.stack([-sz, cz], 1)], 0)
    pair = pair.reshape(2, K, 2, slabs, depth)
    fwd_z = np.einsum("akbsd,gh,pq->gpakshdbq", pair, np.eye(groups), np.eye(lift))
    fwd_z = fwd_z.reshape(groups * lift * 2 * K, slabs * rows * lift)
    tile = np.kron(np.eye(8), np.tile(np.eye(K), (1, half)))
    total = np.kron(np.eye(width), np.ones((1, half)))
    double = np.where(np.arange(K) == 0, 1.0, 2.0)[:, None]
    dz, ez = cz * double, sz * double
    back = np.stack([np.stack([dz, -ez], 0), np.stack([ez, dz], 0)], 0)
    back = back.reshape(2, 2, K, slabs, depth).transpose(3, 4, 0, 1, 2)
    back_z = np.broadcast_to(back[:, :, :, :, None, :], (slabs, depth, 2, 2, half, K))
    back_z = back_z.reshape(whole_z * 2, 2 * half * K).T
    order = np.arange(groups * lift * whole_z * 2).reshape(groups, lift, slabs, depth, 2)
    order = order.transpose(2, 0, 3, 4, 1).ravel()
    leave = np.eye(order.size)[order]
    back_x = np.block([[cx.T, -sx.T], [sx.T, cx.T]])
    back_y = np.concatenate([np.kron(eye4, cy), np.kron(eye4, -sy)], 0)
    named = dict(
        fwd_y=fwd_y, fwd_x=fwd_x, spread=spread, collect=collect, fwd_z=fwd_z, tile=tile,
        total=total, expand=total.T, back_z=back_z, leave=leave, back_x=back_x, back_y=back_y,
    )
    return {name: np.ascontiguousarray(value).astype(BF) for name, value in named.items()}


def mm(a, b):
    return jnp.dot(a, b, preferred_element_type=jnp.float32)


def mask_of(half):
    row = lax.broadcasted_iota(jnp.int32, (4 * half, half * K), 0) % half
    column = lax.broadcasted_iota(jnp.int32, (4 * half, half * K), 1) // K
    return row == column


def lift_body(fields, kron, bias, hidden):
    width, depth, nx, ny = hidden.shape
    for z in range(depth):
        for g in range(nx // 16):
            block = fields[:, z, g * 16 : g * 16 + 16, :].reshape(-1, ny)
            value = mm(kron[...], block).reshape(width, 16, ny) + bias[...]
            hidden[:, z, g * 16 : g * 16 + 16, :] = value.astype(jnp.bfloat16)


def forward_body(hidden, fwd_y, fwd_x, spread, local, out):
    width, depth, nx, ny = hidden.shape
    for g in range(width // 4):
        for z in range(depth):
            block = jnp.concatenate([hidden[4 * g + c, z] for c in range(4)], axis=1)
            along = (mm(block, fwd_y[...]) * (1.0 / math.sqrt(ny))).astype(jnp.bfloat16)
            lanes = along.shape[1] // 2
            along = jnp.concatenate([along[:, :lanes], along[:, lanes:]], axis=0)
            spec = mm(fwd_x[...], along) * (1.0 / math.sqrt(nx))
            at = (g * depth + z) * spec.shape[0]
            local[at : at + spec.shape[0], :] = spec.astype(jnp.bfloat16)
    out[...] = mm(spread[...], local[...]).astype(jnp.bfloat16)


def modes_body(place, got, fwd_z, tile, total, modes, held, scale):
    half = 2 * K
    lanes = half * K
    width = modes.shape[1]
    lift = modes.shape[2] // lanes
    mask = mask_of(half)
    flat = (mm(fwd_z[...], got[...]) * scale).T.astype(jnp.bfloat16)
    per = lift * 2
    for b in range(flat.shape[1] // 128):
        wide = mm(flat[:, b * 128 : b * 128 + 128], tile[...])
        for e in range(8):
            g, pr = divmod(b * 8 + e, per)
            piece = jnp.where(mask, wide[:, e * lanes : (e + 1) * lanes], 0.0)
            held[pr, g * 128 : g * 128 + 128, :] = piece.astype(jnp.bfloat16)
    for p in range(lift):
        for r in range(2):
            value = mm(total[...], held[p * 2 + r])
            if p == 0:
                lane = lax.broadcasted_iota(jnp.int32, value.shape, 1)
                value = jnp.where(lane + place == 0, 0.0, value)
            modes[r, :, p * lanes : (p + 1) * lanes] = value.astype(jnp.bfloat16)


def mix_body(modes, weights, mixed):
    variants, _, width, lanes = modes.shape
    step = 256
    for b in range(lanes // step):
        at = slice(b * step, (b + 1) * step)
        rows = [[modes[m, r, :, at].astype(jnp.float32) for r in range(2)] for m in range(variants)]
        sums = [[0.0, 0.0] for _ in range(variants)]
        for i in range(width):
            wr = weights[0, i, :, at].astype(jnp.float32)
            wi = weights[1, i, :, at].astype(jnp.float32)
            for m in range(variants):
                real, imag = rows[m][0][i : i + 1], rows[m][1][i : i + 1]
                sums[m][0] += real * wr - imag * wi
                sums[m][1] += imag * wr + real * wi
        for m in range(variants):
            for r in range(2):
                mixed[m, r, :, at] = sums[m][r].astype(jnp.bfloat16)


def planes_body(mixed, expand, back_z, leave, out, local):
    half = 2 * K
    lanes = half * K
    mask = mask_of(half)
    sections = mixed.shape[0]
    lift = mixed.shape[3] // lanes
    groups = expand.shape[0] // 128
    many = back_z.shape[1]
    wholes = [
        jnp.concatenate([mixed[s, r] for s in range(sections)], axis=0) for r in range(2)
    ]
    for g in range(groups):
        values = []
        for p in range(lift):
            pieces = []
            for r in range(2):
                part = wholes[r][:, p * lanes : (p + 1) * lanes]
                wide = mm(expand[g * 128 : g * 128 + 128, :], part)
                pieces.append(jnp.where(mask, wide, 0.0).astype(jnp.bfloat16))
            values.append(mm(jnp.concatenate(pieces, axis=1), back_z[...]) * 0.25)
        value = jnp.concatenate(values, axis=1).T
        local[g * lift * many : (g + 1) * lift * many, :] = value.astype(jnp.bfloat16)
    out[...] = mm(leave[...], local[...]).astype(jnp.bfloat16)


def bypass_body(hidden, kron, bias, direct):
    width, depth, nx, ny = hidden.shape
    for z in range(depth):
        for g in range(nx // 16):
            block = hidden[:, z, g * 16 : g * 16 + 16, :].reshape(-1, ny)
            value = mm(kron[...], block).reshape(width, 16, ny) + bias[...]
            direct[:, z, g * 16 : g * 16 + 16, :] = value


def backward_body(got, direct, collect, back_x, back_y, local, out):
    width, depth, nx, ny = out.shape
    many = back_x.shape[1]
    local[...] = mm(collect[...], got[...]).astype(jnp.bfloat16)
    for g in range(width // 4):
        for z in range(depth):
            at = (g * depth + z) * many
            along = (mm(back_x[...], local[at : at + many, :]) * 0.125).astype(jnp.bfloat16)
            along = jnp.concatenate([along[:nx], along[nx:]], axis=1)
            field = mm(along, back_y[...]) * 0.125
            for c in range(4):
                value = direct[4 * g + c, z] + field[:, c * ny : (c + 1) * ny]
                inner = value * (0.7978845608028654 + 0.035677408136300125 * (value * value))
                value = 0.5 * value * (1.0 + jnp.tanh(inner))
                out[4 * g + c, z] = value.astype(jnp.bfloat16)


def widen(weight, copies):
    ins, outs = weight.shape

    def rep(n):
        row = lax.broadcasted_iota(jnp.int32, (n * copies, n), 0) // copies
        column = lax.broadcasted_iota(jnp.int32, (n * copies, n), 1)
        return (row == column).astype(jnp.bfloat16)

    def last(a, b):
        return lax.dot_general(a, b, (((1,), (1,)), ((), ())), preferred_element_type=jnp.float32)

    tall = last(rep(outs), weight).astype(jnp.bfloat16)
    wide = last(tall, rep(ins))
    row = lax.broadcasted_iota(jnp.int32, wide.shape, 0) % copies
    column = lax.broadcasted_iota(jnp.int32, wide.shape, 1) % copies
    return jnp.where(row == column, wide, 0.0).astype(jnp.bfloat16)


def start_kernel(fields, lift_weight, lift_bias, fwd_y, fwd_x, spread, hidden, out, kron, local):
    kron[...] = widen(lift_weight[...], 16)
    lift_body(fields, kron, lift_bias, hidden)
    forward_body(hidden, fwd_y, fwd_x, spread, local, out)


def layer_kernel(
    got, hidden, weight, bias, collect, back_x, back_y, fwd_y, fwd_x, spread,
    new, out, kron, direct, local,
):
    kron[...] = widen(weight[...], 16)
    bypass_body(hidden, kron, bias, direct)
    backward_body(got, direct, collect, back_x, back_y, local, new)
    forward_body(new, fwd_y, fwd_x, spread, local, out)


def last_kernel(got, hidden, weight, bias, collect, back_x, back_y, new, kron, direct, local):
    kron[...] = widen(weight[...], 16)
    bypass_body(hidden, kron, bias, direct)
    backward_body(got, direct, collect, back_x, back_y, local, new)


def call(kernel, outs, scratch, *args):
    return pl.pallas_call(
        kernel,
        out_shape=outs,
        in_specs=[pl.BlockSpec(memory_space=pltpu.VMEM)] * len(args),
        out_specs=jax.tree.map(lambda _: pl.BlockSpec(memory_space=pltpu.VMEM), outs),
        scratch_shapes=scratch,
        compiler_params=pltpu.CompilerParams(vmem_limit_bytes=28 * 1024 * 1024),
    )(*args)


def exchange(source, target, rows, send, recv):
    slabs = lax.axis_size("slab")
    me = lax.axis_index("slab")
    mine = pl.ds(pl.multiple_of(me * rows, rows), rows)
    copies = []
    for d in range(1, slabs):
        to = lax.rem(me + d, slabs)
        copies.append(
            pltpu.make_async_remote_copy(
                src_ref=source.at[pl.ds(pl.multiple_of(to * rows, rows), rows)],
                dst_ref=target.at[mine],
                send_sem=send.at[d],
                recv_sem=recv.at[d],
                device_id={"slab": to},
                device_id_type=pl.DeviceIdType.MESH,
            )
        )
        copies[-1].start()
    target[mine, :] = source[mine, :]
    for copy in copies:
        copy.wait()


def middle_kernel(
    layer, scale, spec, weights, fwd_z, tile, total, expand, back_z, leave, out,
    got, held, modes, wide, mixed, joined, local, planes, back,
    weight_sem, send_a, recv_a, send_b, recv_b, send_c, recv_c, send_d, recv_d,
):
    slabs, sections = lax.axis_size("slab"), lax.axis_size("section")
    me, section = lax.axis_index("slab"), lax.axis_index("section")
    rows = spec.shape[0] // slabs
    load = pltpu.make_async_copy(weights.at[layer], wide, weight_sem)
    load.start()
    barrier = pltpu.get_barrier_semaphore()
    for d in range(1, slabs):
        pl.semaphore_signal(
            barrier, inc=1, device_id={"slab": lax.rem(me + d, slabs)},
            device_id_type=pl.DeviceIdType.MESH,
        )
    for e in range(1, sections):
        pl.semaphore_signal(
            barrier, inc=1, device_id={"section": lax.rem(section + e, sections)},
            device_id_type=pl.DeviceIdType.MESH,
        )
    pl.semaphore_wait(barrier, slabs + sections - 2)
    exchange(spec, got, rows, send_a, recv_a)
    modes_body(me, got, fwd_z, tile, total, modes.at[0], held, scale)
    copies = []
    for e in range(1, sections):
        copies.append(
            pltpu.make_async_remote_copy(
                src_ref=modes.at[0],
                dst_ref=modes.at[e],
                send_sem=send_b.at[e],
                recv_sem=recv_b.at[e],
                device_id={"section": lax.rem(section + e, sections)},
                device_id_type=pl.DeviceIdType.MESH,
            )
        )
        copies[-1].start()
    load.wait()
    mix_body(modes.at[0:1], wide, mixed.at[0:1])
    joined[section] = mixed[0]
    for copy in copies:
        copy.wait()
    copies = []
    for e in range(1, sections):
        mix_body(modes.at[e : e + 1], wide, mixed.at[e : e + 1])
        copies.append(
            pltpu.make_async_remote_copy(
                src_ref=mixed.at[e],
                dst_ref=joined.at[section],
                send_sem=send_c.at[e],
                recv_sem=recv_c.at[e],
                device_id={"section": lax.rem(section + sections - e, sections)},
                device_id_type=pl.DeviceIdType.MESH,
            )
        )
        copies[-1].start()
    for copy in copies:
        copy.wait()
    planes_body(joined, expand, back_z, leave, planes, local)
    exchange(planes, back, rows, send_d, recv_d)
    out[...] = back[...]


def middle(layer, spec, weights, t, slabs, sections, depth):
    bf = jnp.bfloat16
    _, _, width, outs, lanes = weights.shape
    half = 2 * K
    share = pltpu.VMEM(spec.shape, bf)
    vmem = pl.BlockSpec(memory_space=pltpu.VMEM)
    tables = [t[name] for name in ("fwd_z", "tile", "total", "expand", "back_z", "leave")]
    dma = pltpu.SemaphoreType.DMA
    return pl.pallas_call(
        functools.partial(middle_kernel, layer, 1.0 / math.sqrt(slabs * depth)),
        out_shape=jax.ShapeDtypeStruct(spec.shape, bf),
        in_specs=[vmem, pl.BlockSpec(memory_space=pl.ANY)] + [vmem] * len(tables),
        out_specs=vmem,
        scratch_shapes=[
            share,
            pltpu.VMEM((lanes // (half * K) * 2, width * half, half * K), bf),
            pltpu.VMEM((sections, 2, width, lanes), bf),
            pltpu.VMEM((2, width, outs, lanes), bf),
            pltpu.VMEM((sections, 2, outs, lanes), bf),
            pltpu.VMEM((sections, 2, outs, lanes), bf),
            share,
            share,
            share,
            dma,
            dma((slabs,)),
            dma((slabs,)),
            dma((sections,)),
            dma((sections,)),
            dma((sections,)),
            dma((sections,)),
            dma((slabs,)),
            dma((slabs,)),
        ],
        compiler_params=pltpu.CompilerParams(
            collective_id=layer, has_side_effects=True, vmem_limit_bytes=28 * 1024 * 1024
        ),
    )(spec, weights, *tables)


def on_device_fast(fields, lift_weight, lift_bias, spectral_weight, bypass_weight, bypass_bias):
    slabs, sections = lax.axis_size("slab"), lax.axis_size("section")
    _, inputs, depth, nx, ny = fields.shape
    width = lift_weight.shape[1]
    half = 2 * K
    bf = jnp.bfloat16
    t = constants(slabs, depth, nx, ny, width)
    t = {name: jnp.asarray(value) for name, value in t.items()}
    rows = width // 4 * depth * 2 * half

    def spread_bias(b):
        return jnp.broadcast_to(b.astype(jnp.float32)[..., None, None], b.shape + (1, ny))

    kron = pltpu.VMEM((width * 16, width * 16), bf)
    local = pltpu.VMEM((rows, 128), bf)
    spec = jax.ShapeDtypeStruct((rows, 128), bf)
    hid = jax.ShapeDtypeStruct((width, depth, nx, ny), bf)
    direct = pltpu.VMEM((width, depth, nx, ny), jnp.float32)
    bias = spread_bias(bypass_bias)
    hidden, out = call(
        start_kernel, (hid, spec), [pltpu.VMEM((width * 16, inputs * 16), bf), local],
        fields[0], lift_weight, spread_bias(lift_bias), t["fwd_y"], t["fwd_x"], t["spread"],
    )
    for layer in range(LAYERS):
        got = middle(layer, out, spectral_weight, t, slabs, sections, depth)
        if layer < LAYERS - 1:
            hidden, out = call(
                layer_kernel, (hid, spec), [kron, direct, local], got, hidden,
                bypass_weight[layer], bias[layer], t["collect"], t["back_x"], t["back_y"],
                t["fwd_y"], t["fwd_x"], t["spread"],
            )
        else:
            hidden = call(
                last_kernel, hid, [kron, direct, local], got, hidden,
                bypass_weight[layer], bias[layer], t["collect"], t["back_x"], t["back_y"],
            )
    return hidden[None]


def solution(mesh):
    slabs, sections = mesh.shape["slab"], mesh.shape["section"]
    placed = (
        P("section", None, "slab", None, None),
        P(),
        P(),
        P(None, None, None, "section", "slab"),
        P(),
        P(),
    )
    fits = 2 * K % slabs == 0

    def whole(fields, *rest):
        single = fits and fields.shape[0] == sections
        return jax.shard_map(
            on_device_fast if single else on_device,
            mesh=mesh,
            in_specs=placed,
            out_specs=P("section", None, "slab", None, None),
            check_vma=False,
        )(fields, *rest)

    return whole
```

```python
import functools
import math

import jax
import jax.numpy as jnp
import ml_dtypes
import numpy as np
from jax import lax
from jax.experimental import pallas as pl
from jax.experimental.pallas import tpu as pltpu
from jax.sharding import PartitionSpec as P

K = 16
LAYERS = 2


def signed_list(count):
    base = jnp.arange(2 * count, dtype=jnp.int32)
    return jnp.where(base < count, base, base - 2 * count)


def tables(freqs, length, span):
    freq = (freqs % length)[:, None]
    where = jnp.arange(span, dtype=jnp.int32)[None, :]
    phase = (freq * where % length).astype(jnp.float32) * (2.0 * math.pi / length)
    return (jnp.cos(phase).astype(jnp.bfloat16), jnp.sin(phase).astype(jnp.bfloat16))


def forward_pair(freqs, length):
    cosine, sine = tables(freqs, length, length)
    return jnp.concatenate([cosine, -sine], axis=0).T


def inverse_planes(mixed, cosine, sine):
    plain = jnp.einsum("mcrjk,kz->mcrjz", mixed, cosine, preferred_element_type=jnp.float32)
    skewed = jnp.einsum("mcrjk,kz->mcrjz", mixed, sine, preferred_element_type=jnp.float32)
    joined = jnp.stack([plain[:, :, 0] - skewed[:, :, 1], skewed[:, :, 0] + plain[:, :, 1]], 2)
    return (joined * 0.25).astype(jnp.bfloat16)


def on_device(fields, lift_weight, lift_bias, spectral_weight, bypass_weight, bypass_bias):
    slabs = lax.axis_size("slab")
    batch, inputs, depth, rows_x, rows_y = fields.shape
    width = lift_weight.shape[1]
    whole_z = depth * slabs
    half = 2 * K
    modes_xy = half * half
    owned = modes_xy // slabs
    place = lax.axis_index("slab")
    hidden = (
        jnp.einsum("mczxy,cd->mdzxy", fields, lift_weight, preferred_element_type=jnp.float32)
        + lift_bias.astype(jnp.float32)[None, :, None, None, None]
    ).astype(jnp.bfloat16)
    xy_list = signed_list(K)
    z_list = jnp.arange(K, dtype=jnp.int32)
    table_y = forward_pair(xy_list, rows_y)
    table_x = forward_pair(xy_list, rows_x)
    table_z = forward_pair(z_list, whole_z)
    doubling = jnp.where(z_list == 0, 1.0, 2.0).astype(jnp.bfloat16)[:, None]
    cos_z, sin_z = tables(z_list, whole_z, whole_z)
    cos_z = cos_z * doubling
    sin_z = sin_z * doubling
    cos_x, sin_x = tables(xy_list, rows_x, rows_x)
    cos_y, sin_y = tables(xy_list, rows_y, rows_y)
    back_y = jnp.concatenate([cos_y, -sin_y], axis=0)
    combined_x = jnp.stack([jnp.stack([cos_x, sin_x], 1), jnp.stack([-sin_x, cos_x], 1)], 0)
    index_modes = place * (owned * K) + jnp.arange(owned * K, dtype=jnp.int32)
    keep = (index_modes != 0).astype(jnp.float32).reshape(owned, K)
    scale_z = 1.0 / math.sqrt(whole_z)
    highest = lax.Precision.HIGHEST
    for layer in range(LAYERS):
        spectral = lax.all_gather(spectral_weight[layer], "section", axis=2, tiled=True)
        along_y = (
            jnp.dot(hidden, table_y, preferred_element_type=jnp.float32) / math.sqrt(rows_y)
        ).astype(jnp.bfloat16)
        both = jnp.einsum("mczxq,xp->mczpq", along_y, table_x, preferred_element_type=jnp.float32)
        spec_real = both[..., :half, :half] - both[..., half:, half:]
        spec_imag = both[..., :half, half:] + both[..., half:, :half]
        spectrum = (jnp.stack([spec_real, spec_imag], 2) / math.sqrt(rows_x)).astype(jnp.bfloat16)
        spectrum = spectrum.reshape(batch, width, 2, depth, modes_xy).transpose(0, 1, 2, 4, 3)
        gathered = lax.all_to_all(spectrum, "slab", split_axis=3, concat_axis=4, tiled=True)
        along_z = jnp.einsum(
            "mcrjz,zq->mcrjq", gathered, table_z, preferred_element_type=jnp.float32
        )
        mode_real = (along_z[:, :, 0, :, :K] - along_z[:, :, 1, :, K:]) * scale_z * keep
        mode_imag = (along_z[:, :, 1, :, :K] + along_z[:, :, 0, :, K:]) * scale_z * keep
        weights = spectral.astype(jnp.float32).reshape(2, width, width, owned, K)
        mixed_real = jnp.einsum(
            "mijk,iojk->mojk", mode_real, weights[0], precision=highest
        ) - jnp.einsum("mijk,iojk->mojk", mode_imag, weights[1], precision=highest)
        mixed_imag = jnp.einsum(
            "mijk,iojk->mojk", mode_imag, weights[0], precision=highest
        ) + jnp.einsum("mijk,iojk->mojk", mode_real, weights[1], precision=highest)
        mixed = jnp.stack([mixed_real, mixed_imag], 2).astype(jnp.bfloat16)
        every_plane = inverse_planes(mixed, cos_z, sin_z)
        planes_back = lax.all_to_all(every_plane, "slab", split_axis=4, concat_axis=3, tiled=True)
        grid = planes_back.reshape(batch, width, 2, half, half, depth)
        along_x = (
            jnp.einsum("mcrpqz,rpsx->mczxsq", grid, combined_x, preferred_element_type=jnp.float32)
            * 0.125
        ).astype(jnp.bfloat16)
        along_x = along_x.reshape(batch, width, depth, rows_x, 2 * half)
        spectral_field = jnp.dot(along_x, back_y, preferred_element_type=jnp.float32) * 0.125
        bypassed = (
            jnp.einsum(
                "mczxy,co->mozxy", hidden, bypass_weight[layer], preferred_element_type=jnp.float32
            )
            + bypass_bias[layer].astype(jnp.float32)[None, :, None, None, None]
        )
        hidden = jax.nn.gelu(bypassed + spectral_field, approximate=True).astype(jnp.bfloat16)
    return hidden


BF = ml_dtypes.bfloat16


def host_tables(freqs, length):
    phase = (freqs[:, None] * np.arange(length)[None, :]) % length * (2.0 * math.pi / length)
    return (
        np.cos(phase).astype(BF).astype(np.float64),
        np.sin(phase).astype(BF).astype(np.float64),
    )


def constants(slabs, depth, nx, ny, width):
    whole_z = slabs * depth
    half = 2 * K
    lift = half // slabs
    groups = width // 4
    signed = np.where(np.arange(half) < K, np.arange(half), np.arange(half) - half)
    cy, sy = host_tables(signed, ny)
    cx, sx = host_tables(signed, nx)
    cz, sz = host_tables(np.arange(K), whole_z)
    eye4 = np.eye(4)
    fwd_y = np.concatenate([np.kron(eye4, cy.T), np.kron(eye4, -sy.T)], 1)
    fwd_x = np.block([[cx, sx], [-sx, cx]])
    rows = groups * depth * 2
    order = np.arange(rows * half).reshape(rows, slabs, lift).transpose(1, 0, 2).ravel()
    spread = np.eye(rows * half)[order]
    collect = spread.T
    pair = np.stack([np.stack([cz, sz], 1), np.stack([-sz, cz], 1)], 0)
    pair = pair.reshape(2, K, 2, slabs, depth)
    fwd_z = np.einsum("akbsd,gh,pq->gpakshdbq", pair, np.eye(groups), np.eye(lift))
    fwd_z = fwd_z.reshape(groups * lift * 2 * K, slabs * rows * lift)
    tile = np.kron(np.eye(8), np.tile(np.eye(K), (1, half)))
    total = np.kron(np.eye(width), np.ones((1, half)))
    double = np.where(np.arange(K) == 0, 1.0, 2.0)[:, None]
    dz, ez = cz * double, sz * double
    back = np.stack([np.stack([dz, -ez], 0), np.stack([ez, dz], 0)], 0)
    back = back.reshape(2, 2, K, slabs, depth).transpose(3, 4, 0, 1, 2)
    back_z = np.broadcast_to(back[:, :, :, :, None, :], (slabs, depth, 2, 2, half, K))
    back_z = back_z.reshape(whole_z * 2, 2 * half * K).T
    order = np.arange(groups * lift * whole_z * 2).reshape(groups, lift, slabs, depth, 2)
    order = order.transpose(2, 0, 3, 4, 1).ravel()
    leave = np.eye(order.size)[order]
    back_x = np.block([[cx.T, -sx.T], [sx.T, cx.T]])
    back_y = np.concatenate([np.kron(eye4, cy), np.kron(eye4, -sy)], 0)
    named = dict(
        fwd_y=fwd_y, fwd_x=fwd_x, spread=spread, collect=collect, fwd_z=fwd_z, tile=tile,
        total=total, expand=total.T, back_z=back_z, leave=leave, back_x=back_x, back_y=back_y,
    )
    return {name: np.ascontiguousarray(value).astype(BF) for name, value in named.items()}


def mm(a, b):
    return jnp.dot(a, b, preferred_element_type=jnp.float32)


def mask_of(half):
    row = lax.broadcasted_iota(jnp.int32, (4 * half, half * K), 0) % half
    column = lax.broadcasted_iota(jnp.int32, (4 * half, half * K), 1) // K
    return row == column


def lift_body(fields, kron, bias, hidden):
    width, depth, nx, ny = hidden.shape
    for z in range(depth):
        for g in range(nx // 16):
            block = fields[:, z, g * 16 : g * 16 + 16, :].reshape(-1, ny)
            value = mm(kron[...], block).reshape(width, 16, ny) + bias[...]
            hidden[:, z, g * 16 : g * 16 + 16, :] = value.astype(jnp.bfloat16)


def forward_body(hidden, fwd_y, fwd_x, spread, local, out):
    width, depth, nx, ny = hidden.shape
    for g in range(width // 4):
        for z in range(depth):
            block = jnp.concatenate([hidden[4 * g + c, z] for c in range(4)], axis=1)
            along = (mm(block, fwd_y[...]) * (1.0 / math.sqrt(ny))).astype(jnp.bfloat16)
            lanes = along.shape[1] // 2
            along = jnp.concatenate([along[:, :lanes], along[:, lanes:]], axis=0)
            spec = mm(fwd_x[...], along) * (1.0 / math.sqrt(nx))
            at = (g * depth + z) * spec.shape[0]
            local[at : at + spec.shape[0], :] = spec.astype(jnp.bfloat16)
    out[...] = mm(spread[...], local[...]).astype(jnp.bfloat16)


def modes_body(place, got, fwd_z, tile, total, modes, held, scale):
    half = 2 * K
    lanes = half * K
    width = modes.shape[1]
    lift = modes.shape[2] // lanes
    mask = mask_of(half)
    flat = (mm(fwd_z[...], got[...]) * scale).T.astype(jnp.bfloat16)
    per = lift * 2
    for b in range(flat.shape[1] // 128):
        wide = mm(flat[:, b * 128 : b * 128 + 128], tile[...])
        for e in range(8):
            g, pr = divmod(b * 8 + e, per)
            piece = jnp.where(mask, wide[:, e * lanes : (e + 1) * lanes], 0.0)
            held[pr, g * 128 : g * 128 + 128, :] = piece.astype(jnp.bfloat16)
    for p in range(lift):
        for r in range(2):
            value = mm(total[...], held[p * 2 + r])
            if p == 0:
                lane = lax.broadcasted_iota(jnp.int32, value.shape, 1)
                value = jnp.where(lane + place == 0, 0.0, value)
            modes[r, :, p * lanes : (p + 1) * lanes] = value.astype(jnp.bfloat16)


def mix_body(modes, weights, mixed):
    variants, _, width, lanes = modes.shape
    step = 256
    for b in range(lanes // step):
        at = slice(b * step, (b + 1) * step)
        rows = [[modes[m, r, :, at].astype(jnp.float32) for r in range(2)] for m in range(variants)]
        sums = [[0.0, 0.0] for _ in range(variants)]
        for i in range(width):
            wr = weights[0, i, :, at].astype(jnp.float32)
            wi = weights[1, i, :, at].astype(jnp.float32)
            for m in range(variants):
                real, imag = rows[m][0][i : i + 1], rows[m][1][i : i + 1]
                sums[m][0] += real * wr - imag * wi
                sums[m][1] += imag * wr + real * wi
        for m in range(variants):
            for r in range(2):
                mixed[m, r, :, at] = sums[m][r].astype(jnp.bfloat16)


def planes_body(mixed, expand, back_z, leave, out, local):
    half = 2 * K
    lanes = half * K
    mask = mask_of(half)
    sections = mixed.shape[0]
    lift = mixed.shape[3] // lanes
    groups = expand.shape[0] // 128
    many = back_z.shape[1]
    wholes = [
        jnp.concatenate([mixed[s, r] for s in range(sections)], axis=0) for r in range(2)
    ]
    for g in range(groups):
        values = []
        for p in range(lift):
            pieces = []
            for r in range(2):
                part = wholes[r][:, p * lanes : (p + 1) * lanes]
                wide = mm(expand[g * 128 : g * 128 + 128, :], part)
                pieces.append(jnp.where(mask, wide, 0.0).astype(jnp.bfloat16))
            values.append(mm(jnp.concatenate(pieces, axis=1), back_z[...]) * 0.25)
        value = jnp.concatenate(values, axis=1).T
        local[g * lift * many : (g + 1) * lift * many, :] = value.astype(jnp.bfloat16)
    out[...] = mm(leave[...], local[...]).astype(jnp.bfloat16)


def bypass_body(hidden, kron, bias, direct):
    width, depth, nx, ny = hidden.shape
    for z in range(depth):
        for g in range(nx // 16):
            block = hidden[:, z, g * 16 : g * 16 + 16, :].reshape(-1, ny)
            value = mm(kron[...], block).reshape(width, 16, ny) + bias[...]
            direct[:, z, g * 16 : g * 16 + 16, :] = value


def backward_body(got, direct, collect, back_x, back_y, local, out):
    width, depth, nx, ny = out.shape
    many = back_x.shape[1]
    local[...] = mm(collect[...], got[...]).astype(jnp.bfloat16)
    for g in range(width // 4):
        for z in range(depth):
            at = (g * depth + z) * many
            along = (mm(back_x[...], local[at : at + many, :]) * 0.125).astype(jnp.bfloat16)
            along = jnp.concatenate([along[:nx], along[nx:]], axis=1)
            field = mm(along, back_y[...]) * 0.125
            for c in range(4):
                value = direct[4 * g + c, z] + field[:, c * ny : (c + 1) * ny]
                inner = value * (0.7978845608028654 + 0.035677408136300125 * (value * value))
                value = 0.5 * value * (1.0 + jnp.tanh(inner))
                out[4 * g + c, z] = value.astype(jnp.bfloat16)


def widen(weight, copies):
    ins, outs = weight.shape

    def rep(n):
        row = lax.broadcasted_iota(jnp.int32, (n * copies, n), 0) // copies
        column = lax.broadcasted_iota(jnp.int32, (n * copies, n), 1)
        return (row == column).astype(jnp.bfloat16)

    def last(a, b):
        return lax.dot_general(a, b, (((1,), (1,)), ((), ())), preferred_element_type=jnp.float32)

    tall = last(rep(outs), weight).astype(jnp.bfloat16)
    wide = last(tall, rep(ins))
    row = lax.broadcasted_iota(jnp.int32, wide.shape, 0) % copies
    column = lax.broadcasted_iota(jnp.int32, wide.shape, 1) % copies
    return jnp.where(row == column, wide, 0.0).astype(jnp.bfloat16)


def start_kernel(fields, lift_weight, lift_bias, fwd_y, fwd_x, spread, hidden, out, kron, local):
    kron[...] = widen(lift_weight[...], 16)
    lift_body(fields, kron, lift_bias, hidden)
    forward_body(hidden, fwd_y, fwd_x, spread, local, out)


def layer_kernel(
    got, hidden, weight, bias, collect, back_x, back_y, fwd_y, fwd_x, spread,
    new, out, kron, direct, local,
):
    kron[...] = widen(weight[...], 16)
    bypass_body(hidden, kron, bias, direct)
    backward_body(got, direct, collect, back_x, back_y, local, new)
    forward_body(new, fwd_y, fwd_x, spread, local, out)


def last_kernel(got, hidden, weight, bias, collect, back_x, back_y, new, kron, direct, local):
    kron[...] = widen(weight[...], 16)
    bypass_body(hidden, kron, bias, direct)
    backward_body(got, direct, collect, back_x, back_y, local, new)


def call(kernel, outs, scratch, *args):
    return pl.pallas_call(
        kernel,
        out_shape=outs,
        in_specs=[pl.BlockSpec(memory_space=pltpu.VMEM)] * len(args),
        out_specs=jax.tree.map(lambda _: pl.BlockSpec(memory_space=pltpu.VMEM), outs),
        scratch_shapes=scratch,
        compiler_params=pltpu.CompilerParams(vmem_limit_bytes=28 * 1024 * 1024),
    )(*args)


def exchange(source, target, rows, send, recv):
    slabs = lax.axis_size("slab")
    me = lax.axis_index("slab")
    mine = pl.ds(pl.multiple_of(me * rows, rows), rows)
    copies = []
    for d in range(1, slabs):
        to = lax.rem(me + d, slabs)
        copies.append(
            pltpu.make_async_remote_copy(
                src_ref=source.at[pl.ds(pl.multiple_of(to * rows, rows), rows)],
                dst_ref=target.at[mine],
                send_sem=send.at[d],
                recv_sem=recv.at[d],
                device_id={"slab": to},
                device_id_type=pl.DeviceIdType.MESH,
            )
        )
        copies[-1].start()
    target[mine, :] = source[mine, :]
    for copy in copies:
        copy.wait()


def middle_kernel(
    layer, scale, spec, weights, fwd_z_in, tile_in, total_in, expand_in, back_z_in, leave_in, out,
    fwd_z, tile, total, expand, back_z, leave, table_sem, got, held, modes, wide, mixed, joined, local, planes, back,
    weight_sem, send_a, recv_a, send_b, recv_b, send_c, recv_c, send_d, recv_d,
):
    slabs, sections = lax.axis_size("slab"), lax.axis_size("section")
    me, section = lax.axis_index("slab"), lax.axis_index("section")
    rows = spec.shape[0] // slabs
    load = pltpu.make_async_copy(weights.at[layer], wide, weight_sem)
    load.start()
    pairs = (
        (fwd_z_in, fwd_z), (tile_in, tile), (total_in, total),
        (expand_in, expand), (back_z_in, back_z), (leave_in, leave),
    )
    fetches = [
        pltpu.make_async_copy(source, target, table_sem.at[n])
        for n, (source, target) in enumerate(pairs)
    ]
    for fetch in fetches:
        fetch.start()
    barrier = pltpu.get_barrier_semaphore()
    for d in range(1, slabs):
        pl.semaphore_signal(
            barrier, inc=1, device_id={"slab": lax.rem(me + d, slabs)},
            device_id_type=pl.DeviceIdType.MESH,
        )
    for e in range(1, sections):
        pl.semaphore_signal(
            barrier, inc=1, device_id={"section": lax.rem(section + e, sections)},
            device_id_type=pl.DeviceIdType.MESH,
        )
    pl.semaphore_wait(barrier, slabs + sections - 2)
    exchange(spec, got, rows, send_a, recv_a)
    for fetch in fetches:
        fetch.wait()
    modes_body(me, got, fwd_z, tile, total, modes.at[0], held, scale)
    copies = []
    for e in range(1, sections):
        copies.append(
            pltpu.make_async_remote_copy(
                src_ref=modes.at[0],
                dst_ref=modes.at[e],
                send_sem=send_b.at[e],
                recv_sem=recv_b.at[e],
                device_id={"section": lax.rem(section + e, sections)},
                device_id_type=pl.DeviceIdType.MESH,
            )
        )
        copies[-1].start()
    load.wait()
    mix_body(modes.at[0:1], wide, mixed.at[0:1])
    joined[section] = mixed[0]
    for copy in copies:
        copy.wait()
    copies = []
    for e in range(1, sections):
        mix_body(modes.at[e : e + 1], wide, mixed.at[e : e + 1])
        copies.append(
            pltpu.make_async_remote_copy(
                src_ref=mixed.at[e],
                dst_ref=joined.at[section],
                send_sem=send_c.at[e],
                recv_sem=recv_c.at[e],
                device_id={"section": lax.rem(section + sections - e, sections)},
                device_id_type=pl.DeviceIdType.MESH,
            )
        )
        copies[-1].start()
    for copy in copies:
        copy.wait()
    planes_body(joined, expand, back_z, leave, planes, local)
    exchange(planes, back, rows, send_d, recv_d)
    out[...] = back[...]


def middle(layer, spec, weights, t, slabs, sections, depth):
    bf = jnp.bfloat16
    _, _, width, outs, lanes = weights.shape
    half = 2 * K
    share = pltpu.VMEM(spec.shape, bf)
    vmem = pl.BlockSpec(memory_space=pltpu.VMEM)
    tables = [t[name] for name in ("fwd_z", "tile", "total", "expand", "back_z", "leave")]
    dma = pltpu.SemaphoreType.DMA
    return pl.pallas_call(
        functools.partial(middle_kernel, layer, 1.0 / math.sqrt(slabs * depth)),
        out_shape=jax.ShapeDtypeStruct(spec.shape, bf),
        in_specs=[vmem] + [pl.BlockSpec(memory_space=pl.ANY)] * (1 + len(tables)),
        out_specs=vmem,
        scratch_shapes=[
            *(pltpu.VMEM(table.shape, bf) for table in tables),
            dma((len(tables),)),
            share,
            pltpu.VMEM((lanes // (half * K) * 2, width * half, half * K), bf),
            pltpu.VMEM((sections, 2, width, lanes), bf),
            pltpu.VMEM((2, width, outs, lanes), bf),
            pltpu.VMEM((sections, 2, outs, lanes), bf),
            pltpu.VMEM((sections, 2, outs, lanes), bf),
            share,
            share,
            share,
            dma,
            dma((slabs,)),
            dma((slabs,)),
            dma((sections,)),
            dma((sections,)),
            dma((sections,)),
            dma((sections,)),
            dma((slabs,)),
            dma((slabs,)),
        ],
        compiler_params=pltpu.CompilerParams(
            collective_id=layer, has_side_effects=True, vmem_limit_bytes=28 * 1024 * 1024
        ),
    )(spec, weights, *tables)


def on_device_fast(fields, lift_weight, lift_bias, spectral_weight, bypass_weight, bypass_bias):
    slabs, sections = lax.axis_size("slab"), lax.axis_size("section")
    _, inputs, depth, nx, ny = fields.shape
    width = lift_weight.shape[1]
    half = 2 * K
    bf = jnp.bfloat16
    t = constants(slabs, depth, nx, ny, width)
    t = {name: jnp.asarray(value) for name, value in t.items()}
    rows = width // 4 * depth * 2 * half

    def spread_bias(b):
        return jnp.broadcast_to(b.astype(jnp.float32)[..., None, None], b.shape + (1, ny))

    kron = pltpu.VMEM((width * 16, width * 16), bf)
    local = pltpu.VMEM((rows, 128), bf)
    spec = jax.ShapeDtypeStruct((rows, 128), bf)
    hid = jax.ShapeDtypeStruct((width, depth, nx, ny), bf)
    direct = pltpu.VMEM((width, depth, nx, ny), jnp.float32)
    bias = spread_bias(bypass_bias)
    hidden, out = call(
        start_kernel, (hid, spec), [pltpu.VMEM((width * 16, inputs * 16), bf), local],
        fields[0], lift_weight, spread_bias(lift_bias), t["fwd_y"], t["fwd_x"], t["spread"],
    )
    for layer in range(LAYERS):
        got = middle(layer, out, spectral_weight, t, slabs, sections, depth)
        if layer < LAYERS - 1:
            hidden, out = call(
                layer_kernel, (hid, spec), [kron, direct, local], got, hidden,
                bypass_weight[layer], bias[layer], t["collect"], t["back_x"], t["back_y"],
                t["fwd_y"], t["fwd_x"], t["spread"],
            )
        else:
            hidden = call(
                last_kernel, hid, [kron, direct, local], got, hidden,
                bypass_weight[layer], bias[layer], t["collect"], t["back_x"], t["back_y"],
            )
    return hidden[None]


def solution(mesh):
    slabs, sections = mesh.shape["slab"], mesh.shape["section"]
    placed = (
        P("section", None, "slab", None, None),
        P(),
        P(),
        P(None, None, None, "section", "slab"),
        P(),
        P(),
    )
    fits = 2 * K % slabs == 0

    def whole(fields, *rest):
        single = fits and fields.shape[0] == sections
        return jax.shard_map(
            on_device_fast if single else on_device,
            mesh=mesh,
            in_specs=placed,
            out_specs=P("section", None, "slab", None, None),
            check_vma=False,
        )(fields, *rest)

    return whole
```
